512 devices in a mesh: seq: 64 (over z_lo, y, x), tensor: 8 (over z_hi, core).
Axes of the slice: x: 4, y: 8, z: 8 (z_hi: 4, z_lo: 2; z = z_hi * 2 + z_lo), core: 2. Of those that a mesh axis runs over, the one named last changes fastest.
Arguments:
- queries: bfloat16 [4096, 16384], P('tensor', 'seq'), may hold values from -6 to 6
- keys: bfloat16 [4096, 16384], P('tensor', 'seq'), may hold values from -6 to 6
- values: bfloat16 [4096, 16384], P('tensor', 'seq'), may hold values from -6 to 6
- out_weight: bfloat16 [4096, 4096], P('tensor', 'seq'), may hold values from -0.25 to 0.25
- decay: float32 [4096, 16], P('tensor'), may hold values from 0.5 to 500
- residue: float32 [4096, 16], P('tensor'), may hold values from -1.5 to 1.5
- skip: float32 [4096], P('tensor'), may hold values from -1 to 1
Outputs:
- mixed: bfloat16 [4096, 16384], P('tensor', 'seq')
The draws below stay inside these ranges and needn't reach their ends.
All inputs are finite; a program needn't handle non-finite values.
Results may differ from the reference program's by a relative error of at most 0.024.
Values may be sent and summed in bfloat16 or wider, within the bound.
No kernel may reach another device: no remote copies, remote signals or barrier semaphores. Data moves between devices by JAX's collectives and lax.ppermute only.
A program may use at most 64 MiB of HBM per device.

```python
import math
import jax
import jax.numpy as jnp
from jax import lax

D = 4096
MODES = 16
TOKENS = 16384
N_TENSOR = 8


def strengthened(array, own_key, source, target, parts, factor):
    def block_of(dim):
        return (jnp.arange(array.shape[dim]) // (array.shape[dim] // parts)).reshape((-1,) + (1,) * (array.ndim - 1 - dim))

    one_side = jax.random.permutation(own_key, parts)[block_of(target)]
    second = (block_of(target) + parts // 2) % parts
    return jnp.where((block_of(source) == one_side) | (block_of(source) == second), factor * array, array)


def steps_of(rng, dims, pieces, least, top_value):
    level, own = 1.0, jax.random.fold_in(rng, 6)
    for dim, shards_of in pieces:
        heights = jnp.exp(jax.random.uniform(jax.random.fold_in(own, dim), (shards_of,), jnp.float32, least / len(pieces), top_value / len(pieces)))
        level = level * jnp.repeat(heights, dims[dim] // shards_of).reshape([-1 if axis == dim else 1 for axis in range(len(dims))])
    return level


def bell_draw(rng, shape, scale, most, split=(), held_as=jnp.bfloat16):
    level = steps_of(rng, shape, split, -0.22, 0.18) if split else 1.0
    drawn = jax.random.normal(rng, shape, jnp.float32) * scale * level
    return jnp.minimum(jnp.maximum(drawn, -most), most).astype(held_as)


def noise_with(key, dims, scale, most, split, heavy, dtype=jnp.bfloat16):
    values = scale * jax.random.normal(key, dims, jnp.float32)
    if split:
        values = values * steps_of(key, dims, split, -0.22, 0.18)
    return jnp.clip(strengthened(values, jax.random.fold_in(key, 3), *heavy), -most, most).astype(dtype)


def setup_inputs(seed: int = 0) -> dict:
    key_list = jax.random.split(jax.random.key(seed), 8)
    queries = bell_draw(key_list[0], (D, TOKENS), 1.0, 6.0, ((0, 8), (1, 64)))
    keys = bell_draw(key_list[1], (D, TOKENS), 1.0, 6.0, ((0, 8), (1, 64)))
    values = bell_draw(key_list[2], (D, TOKENS), 1.0, 6.0, ((0, 8), (1, 64)))
    out_weight = noise_with(key_list[3], (D, D), D ** -0.5, 0.25, ((0, 8), (1, 64)), (0, 1, 64, 4.0))
    decay = jnp.clip(jnp.exp(math.log(500.0) - 6.9077553 * jax.random.uniform(key_list[4], (D, MODES), jnp.float32) ** steps_of(key_list[4], (D, MODES), ((0, 8),), -0.2, 0.2)), 0.5, 500.0)
    residue = bell_draw(key_list[5], (D, MODES), MODES ** -0.5, 1.5, ((0, 8),), jnp.float32)
    skip = jnp.clip(jax.random.uniform(key_list[6], (D,), jnp.float32, -1.0, 1.0) * steps_of(key_list[6], (D,), ((0, 8),), -0.4, 0.0), -1.0, 1.0)
    return dict(queries=queries, keys=keys, values=values, out_weight=out_weight, decay=decay, residue=residue, skip=skip)


def make_filter(decay, residue, length):
    positions = jnp.arange(length).astype(jnp.float32)
    filt = jnp.zeros((decay.shape[0], length), jnp.float32)
    for mode in range(decay.shape[1]):
        rate = decay[:, mode:mode + 1] / length
        amplitude = residue[:, mode:mode + 1] * jnp.sqrt(2.0 * rate)
        filt = filt + amplitude * jnp.exp(-rate * positions[None, :])
    return filt

def convolve(product, decay, residue, skip):
    length = product.shape[1]
    signal = product.astype(jnp.float32)
    filt = make_filter(decay, residue, length)
    spectrum = jnp.fft.rfft(signal, n=2 * length, axis=1) * jnp.fft.rfft(filt, n=2 * length, axis=1)
    causal = jnp.fft.irfft(spectrum, n=2 * length, axis=1)[:, :length].astype(jnp.float32)
    return (causal + skip[:, None] * signal).astype(jnp.bfloat16)

def reference(queries, keys, values, out_weight, decay, residue, skip):
    product = keys * values
    filtered = convolve(product, decay, residue, skip)
    gated = queries * filtered
    width = out_weight.shape[0]
    group = width // N_TENSOR
    weight_groups = out_weight.reshape(N_TENSOR, group, width)
    gated_groups = gated.reshape(N_TENSOR, group, gated.shape[1])

    def add_group(total, pair):
        weight_rows, gated_rows = pair
        partial_value = jnp.dot(weight_rows.T, gated_rows, preferred_element_type=jnp.float32).astype(jnp.bfloat16)
        return (total + partial_value.astype(jnp.float32), None)
    start = jnp.zeros((width, gated.shape[1]), jnp.float32)
    mixed, unused = lax.scan(add_group, start, (weight_groups, gated_groups))
    return mixed.astype(jnp.bfloat16)
```

```python
import functools

import jax
import jax.numpy as jnp
from jax import lax
from jax.experimental import pallas as pl
from jax.experimental.pallas import tpu as pltpu
from jax.sharding import Mesh, PartitionSpec as P

MODES = 16
TOTAL = 16384
SPAN = 1024
CHUNKS = 8
STEP = SPAN // CHUNKS
WIDE = 128
BLOCK = 256
VMEM = pltpu.CompilerParams(vmem_limit_bytes=40 * 1024 * 1024)
F32 = jnp.float32
BF16 = jnp.bfloat16


def pack_kernel(q_ref, k_ref, v_ref, w_ref, out_ref):
    product = (k_ref[...].astype(F32) * v_ref[...].astype(F32)).T
    out_ref[0, 0:BLOCK, :] = product.astype(BF16)
    out_ref[0, BLOCK : 2 * BLOCK, :] = q_ref[...].astype(F32).T.astype(BF16)
    out_ref[0, 2 * BLOCK :, :] = w_ref[...].astype(F32).T.astype(BF16)


def pack(q, k, v, w):
    rows = lambda width: pl.BlockSpec((WIDE, width), lambda j: (j, 0))
    return pl.pallas_call(
        pack_kernel,
        grid=(4,),
        in_specs=[rows(BLOCK), rows(BLOCK), rows(BLOCK), rows(64)],
        out_specs=pl.BlockSpec((1, 2 * BLOCK + 64, WIDE), lambda j: (j, 0, 0)),
        out_shape=jax.ShapeDtypeStruct((4, 2 * BLOCK + 64, WIDE), BF16),
        compiler_params=VMEM,
        name="pack",
    )(q, k, v, w)


def load_product(moved_ref, p_ref):
    for j in range(4):
        p_ref[BLOCK * j : BLOCK * (j + 1), :] = moved_ref[j, 0:BLOCK, :].astype(F32)


def ends_kernel(moved_ref, rate_ref, ends_ref, sent_ref, p_ref):
    load_product(moved_ref, p_ref)
    rate = rate_ref[...]
    ratio = jnp.exp(-rate)
    ratios = [jnp.broadcast_to(ratio[m : m + 1, :], (CHUNKS, WIDE)) for m in range(MODES)]

    def step(i, states):
        p = p_ref[pl.ds(i, CHUNKS, stride=STEP), :]
        return tuple(h * r + p for h, r in zip(states, ratios))

    zero = jnp.zeros((CHUNKS, WIDE), F32)
    states = lax.fori_loop(0, STEP, step, (zero,) * MODES, unroll=8)
    for m in range(MODES):
        ends_ref[pl.ds(m, CHUNKS, stride=MODES), :] = states[m]
    over_chunk = jnp.exp(-rate * STEP)
    total = ends_ref[0:MODES, :]
    for s in range(1, CHUNKS):
        total = total * over_chunk + ends_ref[MODES * s : MODES * (s + 1), :]
    for g in range(16):
        sent_ref[g] = total


def ends_call(moved, rate):
    return pl.pallas_call(
        ends_kernel,
        out_shape=[
            jax.ShapeDtypeStruct((CHUNKS * MODES, WIDE), F32),
            jax.ShapeDtypeStruct((16, MODES, WIDE), F32),
        ],
        scratch_shapes=[pltpu.VMEM((SPAN, WIDE), F32)],
        compiler_params=VMEM,
        name="ends",
    )(moved, rate)


def scan_kernel(me_ref, moved_ref, rate_ref, amp_ref, skip_ref, ends_ref, got_ref, out_ref, p_ref, y_ref, first_ref):
    load_product(moved_ref, p_ref)
    rate = rate_ref[...]
    me = me_ref[0]
    over_span = jnp.exp(-rate * SPAN)
    over_chunk = jnp.exp(-rate * STEP)
    state = jnp.zeros((MODES, WIDE), F32)
    for g in range(16):
        state = jnp.where(g < me, state * over_span + got_ref[g], state)
    for s in range(CHUNKS):
        first_ref[MODES * s : MODES * (s + 1), :] = state
        state = state * over_chunk + ends_ref[MODES * s : MODES * (s + 1), :]
    ratio = jnp.exp(-rate)
    amp = amp_ref[...]
    spread = lambda x, m: jnp.broadcast_to(x[m : m + 1, :], (CHUNKS, WIDE))
    ratios = [spread(ratio, m) for m in range(MODES)]
    amps = [spread(amp, m) for m in range(MODES)]
    firsts = tuple(first_ref[pl.ds(m, CHUNKS, stride=MODES), :] for m in range(MODES))

    def step(i, states):
        p = p_ref[pl.ds(i, CHUNKS, stride=STEP), :]
        states = tuple(h * r + p for h, r in zip(states, ratios))
        terms = [h * a for h, a in zip(states, amps)]
        while len(terms) > 1:
            terms = [terms[n] + terms[n + 1] for n in range(0, len(terms), 2)]
        y_ref[pl.ds(i, CHUNKS, stride=STEP), :] = terms[0]
        return states

    lax.fori_loop(0, STEP, step, firsts, unroll=8)
    skip = skip_ref[...]
    for j in range(4):
        rows = slice(BLOCK * j, BLOCK * (j + 1))
        filtered = (y_ref[rows, :] + skip * p_ref[rows, :]).astype(BF16)
        gate = moved_ref[j, BLOCK : 2 * BLOCK, :].astype(F32)
        out_ref[rows, :] = (gate * filtered.astype(F32)).astype(BF16)


def scan_call(me, moved, rate, amp, skip, ends, got):
    vmem = pl.BlockSpec(memory_space=pltpu.VMEM)
    return pl.pallas_call(
        scan_kernel,
        in_specs=[pl.BlockSpec(memory_space=pltpu.SMEM)] + [vmem] * 6,
        out_shape=jax.ShapeDtypeStruct((SPAN, WIDE), BF16),
        scratch_shapes=[
            pltpu.VMEM((SPAN, WIDE), F32),
            pltpu.VMEM((SPAN, WIDE), F32),
            pltpu.VMEM((CHUNKS * MODES, WIDE), F32),
        ],
        compiler_params=VMEM,
        name="scan",
    )(me, moved, rate, amp, skip, ends, got)


def project_kernel(zh_ref, w_ref, g0_ref, g1_ref, g2_ref, g3_ref, out_ref):
    zh = zh_ref[0]
    for j in range(4):
        rows = slice(BLOCK * j, BLOCK * (j + 1))
        total = jnp.zeros((512, BLOCK), F32)
        for d, g_ref in enumerate((g0_ref, g1_ref, g2_ref, g3_ref)):
            owner = lax.rem(zh + d, 4)
            for core in range(2):
                weight = w_ref[2 * owner + core]
                total += lax.dot_general(
                    weight, g_ref[core, rows, :], (((1,), (1,)), ((), ())), preferred_element_type=F32
                )
        out_ref[j] = total.astype(BF16)


def project(zh, w, *gated):
    vmem = pl.BlockSpec(memory_space=pltpu.VMEM)
    return pl.pallas_call(
        project_kernel,
        in_specs=[pl.BlockSpec(memory_space=pltpu.SMEM)] + [vmem] * 5,
        out_shape=jax.ShapeDtypeStruct((4, 512, BLOCK), BF16),
        compiler_params=VMEM,
        name="project",
    )(zh, w, *gated)


def gather_weight(block):
    perm = []
    for zl in range(2):
        for y in range(8):
            for t in range(8):
                slot = 2 * t + y % 2
                owner = zl * 4 + y // 2
                perm.append(((zl * 8 + y) * 8 + t, slot * 8 + owner))
    block = lax.ppermute(block, ("zl", "y", "zh", "core"), perm)
    spread = jnp.broadcast_to(block[None], (16,) + block.shape)
    return lax.all_to_all(spread, ("zl", "y"), 0, 0, tiled=True).reshape(8, 512, WIDE)


def per_device(q, k, v, w, decay, residue, skip):
    x = lax.axis_index("x")
    zh = lax.axis_index("zh").reshape(1)
    me = (lax.axis_index("zl") * 8 + lax.axis_index("y")).reshape(1)
    moved = lax.all_to_all(pack(q, k, v, w), "x", 0, 0, tiled=True)
    rate = lax.dynamic_slice_in_dim(decay, x * WIDE, WIDE, 0).T / TOTAL
    amp = lax.dynamic_slice_in_dim(residue, x * WIDE, WIDE, 0).T * jnp.sqrt(2.0 * rate)
    own_skip = lax.dynamic_slice_in_dim(skip, x * WIDE, WIDE, 0)[None]
    weight = gather_weight(moved[:, 2 * BLOCK :, :].reshape(256, WIDE))
    ends, sent = ends_call(moved, rate)
    got = lax.all_to_all(sent, ("zl", "y"), 0, 0, tiled=True)
    gated = scan_call(me, moved, rate, amp, own_skip, ends, got)
    shifted = [gated] + [
        lax.ppermute(gated, "zh", [((n + d) % 4, n) for n in range(4)]) for d in (1, 2, 3)
    ]
    both = [lax.all_gather(g, "core", axis=0, tiled=False) for g in shifted]
    parts = project(zh, weight, *both)
    parts = lax.all_to_all(parts, "x", 0, 0, tiled=True)
    return jnp.sum(parts.astype(F32), axis=0).astype(BF16)


def solution(mesh):
    fine = Mesh(mesh.devices.reshape(2, 8, 4, 4, 2), ("zl", "y", "x", "zh", "core"))
    seq, tensor = ("zl", "y", "x"), ("zh", "core")
    placed = (P(tensor, seq),) * 4 + (P(tensor, None), P(tensor, None), P(tensor))
    return jax.shard_map(
        per_device, mesh=fine, in_specs=placed, out_specs=P(tensor, seq), check_vma=False
    )
```

```python
import jax
import jax.numpy as jnp
from jax import lax
from jax.experimental import pallas as pl
from jax.experimental.pallas import tpu as pltpu
from jax.sharding import Mesh, PartitionSpec as P

MODES = 16
TOTAL = 16384
SPAN = 1024
CHUNKS = 8
STEP = SPAN // CHUNKS
WIDE = 128
BLOCK = 256
VMEM = pltpu.CompilerParams(vmem_limit_bytes=40 * 1024 * 1024)
F32 = jnp.float32
BF16 = jnp.bfloat16


def pack_kernel(q_hbm, k_hbm, v_hbm, w_hbm, out_ref, q_ref, k_ref, v_ref, w_ref, sems):
    pairs = ((k_hbm, k_ref), (v_hbm, v_ref), (q_hbm, q_ref), (w_hbm, w_ref))
    copies = [pltpu.make_async_copy(*pair, sems.at[n]) for n, pair in enumerate(pairs)]
    for copy in copies:
        copy.start()
    copies[0].wait()
    copies[1].wait()
    for j in range(4):
        rows = slice(WIDE * j, WIDE * (j + 1))
        out_ref[j, 0:BLOCK, :] = (k_ref[rows, :] * v_ref[rows, :]).T
    copies[2].wait()
    for j in range(4):
        out_ref[j, BLOCK : 2 * BLOCK, :] = q_ref[WIDE * j : WIDE * (j + 1), :].T
    copies[3].wait()
    for j in range(4):
        out_ref[j, 2 * BLOCK :, :] = w_ref[:, WIDE * j : WIDE * (j + 1)]


def pack(q, k, v, w):
    return pl.pallas_call(
        pack_kernel,
        in_specs=[pl.BlockSpec(memory_space=pltpu.HBM)] * 4,
        out_specs=pl.BlockSpec(memory_space=pltpu.VMEM),
        out_shape=jax.ShapeDtypeStruct((4, 2 * BLOCK + 64, WIDE), BF16),
        scratch_shapes=[pltpu.VMEM((4 * WIDE, BLOCK), BF16)] * 3
        + [pltpu.VMEM((64, 4 * WIDE), BF16), pltpu.SemaphoreType.DMA((4,))],
        compiler_params=pltpu.CompilerParams(vmem_limit_bytes=60 * 1024 * 1024),
        name="pack",
    )(q, k, v, w)


def load_product(moved_ref, p_ref):
    for j in range(4):
        p_ref[BLOCK * j : BLOCK * (j + 1), :] = moved_ref[j, 0:BLOCK, :].astype(F32)


def ends_kernel(moved_ref, rate_ref, ends_ref, sent_ref, p_ref):
    load_product(moved_ref, p_ref)
    rate = rate_ref[...]
    ratio = jnp.exp(-rate)
    ratios = [jnp.broadcast_to(ratio[m : m + 1, :], (CHUNKS, WIDE)) for m in range(MODES)]

    def step(i, states):
        p = p_ref[pl.ds(i, CHUNKS, stride=STEP), :]
        return tuple(h * r + p for h, r in zip(states, ratios))

    zero = jnp.zeros((CHUNKS, WIDE), F32)
    states = lax.fori_loop(0, STEP, step, (zero,) * MODES, unroll=8)
    for m in range(MODES):
        ends_ref[pl.ds(m, CHUNKS, stride=MODES), :] = states[m]
    over_chunk = jnp.exp(-rate * STEP)
    total = ends_ref[0:MODES, :]
    for s in range(1, CHUNKS):
        total = total * over_chunk + ends_ref[MODES * s : MODES * (s + 1), :]
    for g in range(16):
        sent_ref[g] = total


def ends_call(moved, rate):
    return pl.pallas_call(
        ends_kernel,
        out_shape=[
            jax.ShapeDtypeStruct((CHUNKS * MODES, WIDE), F32),
            jax.ShapeDtypeStruct((16, MODES, WIDE), F32),
        ],
        scratch_shapes=[pltpu.VMEM((SPAN, WIDE), F32)],
        compiler_params=VMEM,
        name="ends",
    )(moved, rate)


def scan_kernel(me_ref, moved_ref, rate_ref, amp_ref, skip_ref, ends_ref, got_ref, out_ref, p_ref, y_ref, first_ref):
    load_product(moved_ref, p_ref)
    rate = rate_ref[...]
    me = me_ref[0]
    over_span = jnp.exp(-rate * SPAN)
    over_chunk = jnp.exp(-rate * STEP)
    state = jnp.zeros((MODES, WIDE), F32)
    for g in range(16):
        state = jnp.where(g < me, state * over_span + got_ref[g], state)
    for s in range(CHUNKS):
        first_ref[MODES * s : MODES * (s + 1), :] = state
        state = state * over_chunk + ends_ref[MODES * s : MODES * (s + 1), :]
    ratio = jnp.exp(-rate)
    amp = amp_ref[...]
    spread = lambda x, m: jnp.broadcast_to(x[m : m + 1, :], (CHUNKS, WIDE))
    ratios = [spread(ratio, m) for m in range(MODES)]
    amps = [spread(amp, m) for m in range(MODES)]
    firsts = tuple(first_ref[pl.ds(m, CHUNKS, stride=MODES), :] for m in range(MODES))

    def step(i, states):
        p = p_ref[pl.ds(i, CHUNKS, stride=STEP), :]
        states = tuple(h * r + p for h, r in zip(states, ratios))
        terms = [h * a for h, a in zip(states, amps)]
        while len(terms) > 1:
            terms = [terms[n] + terms[n + 1] for n in range(0, len(terms), 2)]
        y_ref[pl.ds(i, CHUNKS, stride=STEP), :] = terms[0]
        return states

    lax.fori_loop(0, STEP, step, firsts, unroll=8)
    skip = skip_ref[...]
    for j in range(4):
        rows = slice(BLOCK * j, BLOCK * (j + 1))
        filtered = (y_ref[rows, :] + skip * p_ref[rows, :]).astype(BF16)
        gate = moved_ref[j, BLOCK : 2 * BLOCK, :].astype(F32)
        gated = (gate * filtered.astype(F32)).astype(BF16)
        out_ref[rows, :] = gated


def scan_call(me, moved, rate, amp, skip, ends, got):
    vmem = pl.BlockSpec(memory_space=pltpu.VMEM)
    return pl.pallas_call(
        scan_kernel,
        in_specs=[pl.BlockSpec(memory_space=pltpu.SMEM)] + [vmem] * 6,
        out_shape=jax.ShapeDtypeStruct((SPAN, WIDE), BF16),
        scratch_shapes=[
            pltpu.VMEM((SPAN, WIDE), F32),
            pltpu.VMEM((SPAN, WIDE), F32),
            pltpu.VMEM((CHUNKS * MODES, WIDE), F32),
        ],
        compiler_params=VMEM,
        name="scan",
    )(me, moved, rate, amp, skip, ends, got)


def copies_kernel(after_ref, own_ref, far_ref, out_ref):
    del after_ref
    for n in range(8):
        out_ref[n, 0] = own_ref[...]
        out_ref[n, 1] = far_ref[...]


def copies_of(after, own, far):
    vmem = pl.BlockSpec(memory_space=pltpu.VMEM)
    return pl.pallas_call(
        copies_kernel,
        in_specs=[pl.BlockSpec(memory_space=pl.ANY), vmem, vmem],
        out_shape=jax.ShapeDtypeStruct((8, 2, 256, WIDE), BF16),
        compiler_params=VMEM,
        name="copies",
    )(after, own, far)


def project_kernel(place_ref, w_ref, g0_ref, g1_ref, g2_ref, g3_ref, out_ref):
    zh, zl = place_ref[0], place_ref[1]
    half = SPAN // 2
    for h in range(2):
        for part in range(2):
            tokens = slice(half * part, half * (part + 1))
            total = jnp.zeros((256, half), F32)
            for d, g_ref in enumerate((g0_ref, g1_ref, g2_ref, g3_ref)):
                owner = lax.rem(zh + d, 4)
                weights, values = [], []
                for core in range(2):
                    t = 2 * owner + core
                    weights.append(w_ref[2 * lax.rem(t, 4) + h, lax.rem(t // 4 + zl, 2)])
                    values.append(g_ref[core, tokens, :])
                total += lax.dot_general(
                    jnp.concatenate(weights, axis=1),
                    jnp.concatenate(values, axis=1),
                    (((1,), (1,)), ((), ())),
                    preferred_element_type=F32,
                )
            for j in range(2):
                out_ref[2 * part + j, 256 * h : 256 * (h + 1), :] = total[:, BLOCK * j : BLOCK * (j + 1)].astype(BF16)


def project(place, w, *gated):
    vmem = pl.BlockSpec(memory_space=pltpu.VMEM)
    return pl.pallas_call(
        project_kernel,
        in_specs=[pl.BlockSpec(memory_space=pltpu.SMEM)] + [vmem] * 5,
        out_shape=jax.ShapeDtypeStruct((4, 512, BLOCK), BF16),
        compiler_params=VMEM,
        name="project",
    )(place, w, *gated)


def finish_kernel(parts_ref, out_ref):
    total = parts_ref[0].astype(F32)
    for n in range(1, 4):
        total += parts_ref[n].astype(F32)
    out_ref[...] = total.astype(BF16)


def finish(parts):
    return pl.pallas_call(
        finish_kernel,
        out_shape=jax.ShapeDtypeStruct((512, BLOCK), BF16),
        compiler_params=VMEM,
        name="finish",
    )(parts)


def gather_weight(block):
    out = []
    for flip in range(2):
        perm = []
        for zl in range(2):
            for y in range(8):
                for t in range(8):
                    place = (2 * t + y % 2 + 8 * flip) % 16
                    perm.append(((zl * 8 + y) * 8 + t, place * 8 + zl * 4 + y // 2))
        out.append(lax.ppermute(block, ("zl", "y", "zh", "core"), perm))
    return out


def per_device(q, k, v, w, decay, residue, skip):
    x = lax.axis_index("x")
    zh, zl = lax.axis_index("zh"), lax.axis_index("zl")
    me = (zl * 8 + lax.axis_index("y")).reshape(1)
    moved = lax.all_to_all(pack(q, k, v, w.T), "x", 0, 0, tiled=True)
    rate = lax.dynamic_slice_in_dim(decay, x * WIDE, WIDE, 0).T / TOTAL
    amp = lax.dynamic_slice_in_dim(residue, x * WIDE, WIDE, 0).T * jnp.sqrt(2.0 * rate)
    own_skip = lax.dynamic_slice_in_dim(skip, x * WIDE, WIDE, 0)[None]
    ends, sent = ends_call(moved, rate)
    got = lax.all_to_all(sent, ("zl", "y"), 0, 0, tiled=True)
    pieces = gather_weight(moved[:, 2 * BLOCK :, :].reshape(256, WIDE))
    gated = scan_call(me, moved, rate, amp, own_skip, ends, got)
    weight = lax.all_to_all(copies_of(gated, *pieces), "y", 0, 0, tiled=True)
    shifted = [gated] + [
        lax.ppermute(gated, "zh", [((n + d) % 4, n) for n in range(4)]) for d in (1, 2, 3)
    ]
    both = [lax.all_gather(g, "core", axis=0, tiled=False) for g in shifted]
    parts = project(jnp.stack([zh, zl]), weight, *both)
    return finish(lax.all_to_all(parts, "x", 0, 0, tiled=True))


def solution(mesh):
    fine = Mesh(mesh.devices.reshape(2, 8, 4, 4, 2), ("zl", "y", "x", "zh", "core"))
    seq, tensor = ("zl", "y", "x"), ("zh", "core")
    placed = (P(tensor, seq),) * 4 + (P(tensor, None), P(tensor, None), P(tensor))
    return jax.shard_map(
        per_device, mesh=fine, in_specs=placed, out_specs=P(tensor, seq), check_vma=False
    )
```

```python
import jax
import jax.numpy as jnp
from jax import lax
from jax.experimental import pallas as pl
from jax.experimental.pallas import tpu as pltpu
from jax.sharding import Mesh, PartitionSpec as P

MODES = 16
TOTAL = 16384
SPAN = 1024
CHUNKS = 8
STEP = SPAN // CHUNKS
WIDE = 128
BLOCK = 256
VMEM = pltpu.CompilerParams(vmem_limit_bytes=40 * 1024 * 1024)
F32 = jnp.float32
BF16 = jnp.bfloat16


def pack_kernel(q_hbm, k_hbm, v_hbm, w_hbm, out_ref, q_ref, k_ref, v_ref, w_ref, sems):
    pairs = ((k_hbm, k_ref), (v_hbm, v_ref), (q_hbm, q_ref), (w_hbm, w_ref))
    copies = [pltpu.make_async_copy(*pair, sems.at[n]) for n, pair in enumerate(pairs)]
    for copy in copies:
        copy.start()
    copies[0].wait()
    copies[1].wait()
    for j in range(4):
        rows = slice(WIDE * j, WIDE * (j + 1))
        out_ref[j, 0:BLOCK, :] = (k_ref[rows, :] * v_ref[rows, :]).T
    copies[2].wait()
    for j in range(4):
        out_ref[j, BLOCK : 2 * BLOCK, :] = q_ref[WIDE * j : WIDE * (j + 1), :].T
    copies[3].wait()
    for j in range(4):
        out_ref[j, 2 * BLOCK :, :] = w_ref[:, WIDE * j : WIDE * (j + 1)]


def pack(q, k, v, w):
    return pl.pallas_call(
        pack_kernel,
        in_specs=[pl.BlockSpec(memory_space=pltpu.HBM)] * 4,
        out_specs=pl.BlockSpec(memory_space=pltpu.VMEM),
        out_shape=jax.ShapeDtypeStruct((4, 2 * BLOCK + 64, WIDE), BF16),
        scratch_shapes=[pltpu.VMEM((4 * WIDE, BLOCK), BF16)] * 3
        + [pltpu.VMEM((64, 4 * WIDE), BF16), pltpu.SemaphoreType.DMA((4,))],
        compiler_params=pltpu.CompilerParams(vmem_limit_bytes=60 * 1024 * 1024),
        name="pack",
    )(q, k, v, w)


def load_product(moved_ref, p_ref):
    for j in range(4):
        p_ref[BLOCK * j : BLOCK * (j + 1), :] = moved_ref[j, 0:BLOCK, :].astype(F32)


def ends_kernel(moved_ref, rate_ref, ends_ref, sent_ref, p_ref):
    load_product(moved_ref, p_ref)
    rate = rate_ref[...]
    ratio = jnp.exp(-rate)
    ratios = [jnp.broadcast_to(ratio[m : m + 1, :], (CHUNKS, WIDE)) for m in range(MODES)]

    def step(i, states):
        p = p_ref[pl.ds(i, CHUNKS, stride=STEP), :]
        return tuple(h * r + p for h, r in zip(states, ratios))

    zero = jnp.zeros((CHUNKS, WIDE), F32)
    states = lax.fori_loop(0, STEP, step, (zero,) * MODES, unroll=8)
    for m in range(MODES):
        ends_ref[pl.ds(m, CHUNKS, stride=MODES), :] = states[m]
    over_chunk = jnp.exp(-rate * STEP)
    total = ends_ref[0:MODES, :]
    for s in range(1, CHUNKS):
        total = total * over_chunk + ends_ref[MODES * s : MODES * (s + 1), :]
    for g in range(16):
        sent_ref[g] = total


def ends_call(moved, rate):
    return pl.pallas_call(
        ends_kernel,
        out_shape=[
            jax.ShapeDtypeStruct((CHUNKS * MODES, WIDE), F32),
            jax.ShapeDtypeStruct((16, MODES, WIDE), F32),
        ],
        scratch_shapes=[pltpu.VMEM((SPAN, WIDE), F32)],
        compiler_params=VMEM,
        name="ends",
    )(moved, rate)


def scan_kernel(me_ref, moved_ref, rate_ref, amp_ref, skip_ref, ends_ref, got_ref, out_ref, p_ref, y_ref, first_ref):
    load_product(moved_ref, p_ref)
    rate = rate_ref[...]
    me = me_ref[0]
    over_span = jnp.exp(-rate * SPAN)
    over_chunk = jnp.exp(-rate * STEP)
    state = jnp.zeros((MODES, WIDE), F32)
    for g in range(16):
        state = jnp.where(g < me, state * over_span + got_ref[g], state)
    for s in range(CHUNKS):
        first_ref[MODES * s : MODES * (s + 1), :] = state
        state = state * over_chunk + ends_ref[MODES * s : MODES * (s + 1), :]
    ratio = jnp.exp(-rate)
    amp = amp_ref[...]
    spread = lambda x, m: jnp.broadcast_to(x[m : m + 1, :], (CHUNKS, WIDE))
    ratios = [spread(ratio, m) for m in range(MODES)]
    amps = [spread(amp, m) for m in range(MODES)]
    firsts = tuple(first_ref[pl.ds(m, CHUNKS, stride=MODES), :] for m in range(MODES))

    def step(i, states):
        p = p_ref[pl.ds(i, CHUNKS, stride=STEP), :]
        states = tuple(h * r + p for h, r in zip(states, ratios))
        terms = [h * a for h, a in zip(states, amps)]
        while len(terms) > 1:
            terms = [terms[n] + terms[n + 1] for n in range(0, len(terms), 2)]
        y_ref[pl.ds(i, CHUNKS, stride=STEP), :] = terms[0]
        return states

    lax.fori_loop(0, STEP, step, firsts, unroll=8)
    skip = skip_ref[...]
    for j in range(4):
        rows = slice(BLOCK * j, BLOCK * (j + 1))
        filtered = (y_ref[rows, :] + skip * p_ref[rows, :]).astype(BF16)
        gate = moved_ref[j, BLOCK : 2 * BLOCK, :].astype(F32)
        gated = (gate * filtered.astype(F32)).astype(BF16)
        out_ref[rows, :] = gated


def scan_call(me, moved, rate, amp, skip, ends, got):
    vmem = pl.BlockSpec(memory_space=pltpu.VMEM)
    return pl.pallas_call(
        scan_kernel,
        in_specs=[pl.BlockSpec(memory_space=pltpu.SMEM)] + [vmem] * 6,
        out_shape=jax.ShapeDtypeStruct((SPAN, WIDE), BF16),
        scratch_shapes=[
            pltpu.VMEM((SPAN, WIDE), F32),
            pltpu.VMEM((SPAN, WIDE), F32),
            pltpu.VMEM((CHUNKS * MODES, WIDE), F32),
        ],
        compiler_params=VMEM,
        name="scan",
    )(me, moved, rate, amp, skip, ends, got)


def hold_kernel(after_ref, own_ref, out_ref):
    del after_ref
    out_ref[...] = own_ref[...]


def hold(after, own):
    return pl.pallas_call(
        hold_kernel,
        in_specs=[pl.BlockSpec(memory_space=pl.ANY), pl.BlockSpec(memory_space=pltpu.VMEM)],
        out_shape=jax.ShapeDtypeStruct(own.shape, BF16),
        compiler_params=VMEM,
        name="hold",
    )(after, own)


def copies_kernel(own_ref, far_ref, out_ref):
    for n in range(8):
        out_ref[n, 0] = own_ref[...]
        out_ref[n, 1] = far_ref[...]


def copies_of(own, far):
    return pl.pallas_call(
        copies_kernel,
        out_shape=jax.ShapeDtypeStruct((8, 2, 256, WIDE), BF16),
        compiler_params=VMEM,
        name="copies",
    )(own, far)


def project_kernel(place_ref, w_ref, g0_ref, g1_ref, g2_ref, g3_ref, out_ref):
    zh, zl = place_ref[0], place_ref[1]
    half = SPAN // 2
    for h in range(2):
        for part in range(2):
            tokens = slice(half * part, half * (part + 1))
            total = jnp.zeros((256, half), F32)
            for d, g_ref in enumerate((g0_ref, g1_ref, g2_ref, g3_ref)):
                owner = lax.rem(zh + d, 4)
                weights, values = [], []
                for core in range(2):
                    t = 2 * owner + core
                    weights.append(w_ref[2 * lax.rem(t, 4) + h, lax.rem(t // 4 + zl, 2)])
                    values.append(g_ref[core, tokens, :])
                total += lax.dot_general(
                    jnp.concatenate(weights, axis=1),
                    jnp.concatenate(values, axis=1),
                    (((1,), (1,)), ((), ())),
                    preferred_element_type=F32,
                )
            for j in range(2):
                out_ref[2 * part + j, 256 * h : 256 * (h + 1), :] = total[:, BLOCK * j : BLOCK * (j + 1)].astype(BF16)


def project(place, w, *gated):
    vmem = pl.BlockSpec(memory_space=pltpu.VMEM)
    return pl.pallas_call(
        project_kernel,
        in_specs=[pl.BlockSpec(memory_space=pltpu.SMEM)] + [vmem] * 5,
        out_shape=jax.ShapeDtypeStruct((4, 512, BLOCK), BF16),
        compiler_params=VMEM,
        name="project",
    )(place, w, *gated)


def finish_kernel(parts_ref, out_ref):
    total = parts_ref[0].astype(F32)
    for n in range(1, 4):
        total += parts_ref[n].astype(F32)
    out_ref[...] = total.astype(BF16)


def finish(parts):
    return pl.pallas_call(
        finish_kernel,
        out_shape=jax.ShapeDtypeStruct((512, BLOCK), BF16),
        compiler_params=VMEM,
        name="finish",
    )(parts)


def place_weight(block):
    perm = []
    for zl in range(2):
        for y in range(8):
            for t in range(8):
                perm.append(((zl * 8 + y) * 8 + t, (2 * t + y % 2) * 8 + zl * 4 + y // 2))
    return lax.ppermute(block, ("zl", "y", "zh", "core"), perm)


def per_device(q, k, v, w, decay, residue, skip):
    x = lax.axis_index("x")
    zh, zl = lax.axis_index("zh"), lax.axis_index("zl")
    me = (zl * 8 + lax.axis_index("y")).reshape(1)
    moved = lax.all_to_all(pack(q, k, v, w.T), "x", 0, 0, tiled=True)
    rate = lax.dynamic_slice_in_dim(decay, x * WIDE, WIDE, 0).T / TOTAL
    amp = lax.dynamic_slice_in_dim(residue, x * WIDE, WIDE, 0).T * jnp.sqrt(2.0 * rate)
    own_skip = lax.dynamic_slice_in_dim(skip, x * WIDE, WIDE, 0)[None]
    ends, sent = ends_call(moved, rate)
    got = lax.all_to_all(sent, ("zl", "y"), 0, 0, tiled=True)
    own = place_weight(moved[:, 2 * BLOCK :, :].reshape(256, WIDE))
    gated = scan_call(me, moved, rate, amp, own_skip, ends, got)
    far = lax.ppermute(hold(gated, own), "zl", [(0, 1), (1, 0)])
    weight = lax.all_to_all(copies_of(own, far), "y", 0, 0, tiled=True)
    shifted = [gated] + [
        lax.ppermute(gated, "zh", [((n + d) % 4, n) for n in range(4)]) for d in (1, 2, 3)
    ]
    both = [lax.all_gather(g, "core", axis=0, tiled=False) for g in shifted]
    parts = project(jnp.stack([zh, zl]), weight, *both)
    return finish(lax.all_to_all(parts, "x", 0, 0, tiled=True))


def solution(mesh):
    fine = Mesh(mesh.devices.reshape(2, 8, 4, 4, 2), ("zl", "y", "x", "zh", "core"))
    seq, tensor = ("zl", "y", "x"), ("zh", "core")
    placed = (P(tensor, seq),) * 4 + (P(tensor, None), P(tensor, None), P(tensor))
    return jax.shard_map(
        per_device, mesh=fine, in_specs=placed, out_specs=P(tensor, seq), check_vma=False
    )
```

```python
import jax
import jax.numpy as jnp
from jax import lax
from jax.experimental import pallas as pl
from jax.experimental.pallas import tpu as pltpu
from jax.sharding import Mesh, PartitionSpec as P

MODES = 16
TOTAL = 16384
SPAN = 1024
CHUNKS = 8
STEP = SPAN // CHUNKS
WIDE = 128
BLOCK = 256
VMEM = pltpu.CompilerParams(vmem_limit_bytes=40 * 1024 * 1024)
F32 = jnp.float32
BF16 = jnp.bfloat16


def pack_kernel(q_hbm, k_hbm, v_hbm, out_ref, q_ref, k_ref, v_ref, sems):
    pairs = ((k_hbm, k_ref), (v_hbm, v_ref), (q_hbm, q_ref))
    copies = [pltpu.make_async_copy(*pair, sems.at[n]) for n, pair in enumerate(pairs)]
    for copy in copies:
        copy.start()
    copies[0].wait()
    copies[1].wait()
    for j in range(4):
        rows = slice(WIDE * j, WIDE * (j + 1))
        out_ref[j, 0:BLOCK, :] = (k_ref[rows, :] * v_ref[rows, :]).T
    copies[2].wait()
    for j in range(4):
        out_ref[j, BLOCK : 2 * BLOCK, :] = q_ref[WIDE * j : WIDE * (j + 1), :].T


def pack(q, k, v):
    return pl.pallas_call(
        pack_kernel,
        in_specs=[pl.BlockSpec(memory_space=pltpu.HBM)] * 3,
        out_specs=pl.BlockSpec(memory_space=pltpu.VMEM),
        out_shape=jax.ShapeDtypeStruct((4, 2 * BLOCK, WIDE), BF16),
        scratch_shapes=[pltpu.VMEM((4 * WIDE, BLOCK), BF16)] * 3 + [pltpu.SemaphoreType.DMA((3,))],
        compiler_params=pltpu.CompilerParams(vmem_limit_bytes=60 * 1024 * 1024),
        name="pack",
    )(q, k, v)


def load_product(moved_ref, p_ref):
    for j in range(4):
        p_ref[BLOCK * j : BLOCK * (j + 1), :] = moved_ref[j, 0:BLOCK, :].astype(F32)


def ends_kernel(moved_ref, rate_ref, after_ref, ends_ref, sent_ref, p_ref):
    del after_ref
    load_product(moved_ref, p_ref)
    rate = rate_ref[...]
    ratio = jnp.exp(-rate)
    ratios = [jnp.broadcast_to(ratio[m : m + 1, :], (CHUNKS, WIDE)) for m in range(MODES)]

    def step(i, states):
        p = p_ref[pl.ds(i, CHUNKS, stride=STEP), :]
        return tuple(h * r + p for h, r in zip(states, ratios))

    zero = jnp.zeros((CHUNKS, WIDE), F32)
    states = lax.fori_loop(0, STEP, step, (zero,) * MODES, unroll=8)
    for m in range(MODES):
        ends_ref[pl.ds(m, CHUNKS, stride=MODES), :] = states[m]
    over_chunk = jnp.exp(-rate * STEP)
    total = ends_ref[0:MODES, :]
    for s in range(1, CHUNKS):
        total = total * over_chunk + ends_ref[MODES * s : MODES * (s + 1), :]
    for g in range(16):
        sent_ref[g] = total


def ends_call(moved, rate, after):
    vmem = pl.BlockSpec(memory_space=pltpu.VMEM)
    return pl.pallas_call(
        ends_kernel,
        in_specs=[vmem, vmem, pl.BlockSpec(memory_space=pl.ANY)],
        out_shape=[
            jax.ShapeDtypeStruct((CHUNKS * MODES, WIDE), F32),
            jax.ShapeDtypeStruct((16, MODES, WIDE), F32),
        ],
        scratch_shapes=[pltpu.VMEM((SPAN, WIDE), F32)],
        compiler_params=VMEM,
        name="ends",
    )(moved, rate, after)


def scan_kernel(me_ref, moved_ref, rate_ref, amp_ref, skip_ref, ends_ref, got_ref, out_ref, p_ref, y_ref, first_ref):
    load_product(moved_ref, p_ref)
    rate = rate_ref[...]
    me = me_ref[0]
    over_span = jnp.exp(-rate * SPAN)
    over_chunk = jnp.exp(-rate * STEP)
    state = jnp.zeros((MODES, WIDE), F32)
    for g in range(16):
        state = jnp.where(g < me, state * over_span + got_ref[g], state)
    for s in range(CHUNKS):
        first_ref[MODES * s : MODES * (s + 1), :] = state
        state = state * over_chunk + ends_ref[MODES * s : MODES * (s + 1), :]
    ratio = jnp.exp(-rate)
    amp = amp_ref[...]
    spread = lambda x, m: jnp.broadcast_to(x[m : m + 1, :], (CHUNKS, WIDE))
    ratios = [spread(ratio, m) for m in range(MODES)]
    amps = [spread(amp, m) for m in range(MODES)]
    firsts = tuple(first_ref[pl.ds(m, CHUNKS, stride=MODES), :] for m in range(MODES))

    def step(i, states):
        p = p_ref[pl.ds(i, CHUNKS, stride=STEP), :]
        states = tuple(h * r + p for h, r in zip(states, ratios))
        terms = [h * a for h, a in zip(states, amps)]
        while len(terms) > 1:
            terms = [terms[n] + terms[n + 1] for n in range(0, len(terms), 2)]
        y_ref[pl.ds(i, CHUNKS, stride=STEP), :] = terms[0]
        return states

    lax.fori_loop(0, STEP, step, firsts, unroll=8)
    skip = skip_ref[...]
    for j in range(4):
        rows = slice(BLOCK * j, BLOCK * (j + 1))
        filtered = (y_ref[rows, :] + skip * p_ref[rows, :]).astype(BF16)
        gate = moved_ref[j, BLOCK : 2 * BLOCK, :].astype(F32)
        gated = (gate * filtered.astype(F32)).astype(BF16)
        out_ref[rows, :] = gated


def scan_call(me, moved, rate, amp, skip, ends, got):
    vmem = pl.BlockSpec(memory_space=pltpu.VMEM)
    return pl.pallas_call(
        scan_kernel,
        in_specs=[pl.BlockSpec(memory_space=pltpu.SMEM)] + [vmem] * 6,
        out_shape=jax.ShapeDtypeStruct((SPAN, WIDE), BF16),
        scratch_shapes=[
            pltpu.VMEM((SPAN, WIDE), F32),
            pltpu.VMEM((SPAN, WIDE), F32),
            pltpu.VMEM((CHUNKS * MODES, WIDE), F32),
        ],
        compiler_params=VMEM,
        name="scan",
    )(me, moved, rate, amp, skip, ends, got)


def copies_kernel(own_ref, far_ref, out_ref):
    for side, ref in enumerate((own_ref, far_ref)):
        for j in range(4):
            piece = ref[:, WIDE * j : WIDE * (j + 1)]
            for y in range(8):
                out_ref[4 * y + j, side] = piece


def copies_of(own, far):
    return pl.pallas_call(
        copies_kernel,
        out_shape=jax.ShapeDtypeStruct((32, 2, 64, WIDE), BF16),
        compiler_params=VMEM,
        name="copies",
    )(own, far)


def project_kernel(place_ref, w_ref, g0_ref, g1_ref, g2_ref, g3_ref, out_ref):
    zh, zl = place_ref[0], place_ref[1]
    half = SPAN // 2
    for h in range(2):
        for part in range(2):
            tokens = slice(half * part, half * (part + 1))
            total = jnp.zeros((256, half), F32)
            for d, g_ref in enumerate((g0_ref, g1_ref, g2_ref, g3_ref)):
                owner = lax.rem(zh + d, 4)
                weights, values = [], []
                for core in range(2):
                    t = 2 * owner + core
                    place, side = 2 * lax.rem(t, 4) + h, lax.rem(t // 4 + zl, 2)
                    weights.append(jnp.concatenate([w_ref[4 * place + n, side] for n in range(4)], axis=0))
                    values.append(g_ref[core, tokens, :])
                total += lax.dot_general(
                    jnp.concatenate(weights, axis=1),
                    jnp.concatenate(values, axis=1),
                    (((1,), (1,)), ((), ())),
                    preferred_element_type=F32,
                )
            for j in range(2):
                out_ref[2 * part + j, 256 * h : 256 * (h + 1), :] = total[:, BLOCK * j : BLOCK * (j + 1)].astype(BF16)


def project(place, w, *gated):
    vmem = pl.BlockSpec(memory_space=pltpu.VMEM)
    return pl.pallas_call(
        project_kernel,
        in_specs=[pl.BlockSpec(memory_space=pltpu.SMEM)] + [vmem] * 5,
        out_shape=jax.ShapeDtypeStruct((4, 512, BLOCK), BF16),
        compiler_params=VMEM,
        name="project",
    )(place, w, *gated)


def finish_kernel(parts_ref, out_ref):
    total = parts_ref[0].astype(F32)
    for n in range(1, 4):
        total += parts_ref[n].astype(F32)
    out_ref[...] = total.astype(BF16)


def finish(parts):
    return pl.pallas_call(
        finish_kernel,
        out_shape=jax.ShapeDtypeStruct((512, BLOCK), BF16),
        compiler_params=VMEM,
        name="finish",
    )(parts)


def place_weight(block):
    perm = []
    for zl in range(2):
        for y in range(8):
            for t in range(8):
                perm.append(((zl * 8 + y) * 8 + t, (2 * t + y % 2) * 8 + zl * 4 + y // 2))
    return lax.ppermute(block, ("zl", "y", "zh", "core"), perm)


def per_device(q, k, v, w, decay, residue, skip):
    x = lax.axis_index("x")
    zh, zl = lax.axis_index("zh"), lax.axis_index("zl")
    me = (zl * 8 + lax.axis_index("y")).reshape(1)
    own = place_weight(w.T)
    moved = lax.all_to_all(pack(q, k, v), "x", 0, 0, tiled=True)
    rate = lax.dynamic_slice_in_dim(decay, x * WIDE, WIDE, 0).T / TOTAL
    amp = lax.dynamic_slice_in_dim(residue, x * WIDE, WIDE, 0).T * jnp.sqrt(2.0 * rate)
    own_skip = lax.dynamic_slice_in_dim(skip, x * WIDE, WIDE, 0)[None]
    ends, sent = ends_call(moved, rate, own)
    got = lax.all_to_all(sent, ("zl", "y"), 0, 0, tiled=True)
    far = lax.ppermute(own, "zl", [(0, 1), (1, 0)])
    weight = lax.all_to_all(copies_of(own, far), ("y", "x"), 0, 0, tiled=True)
    gated = scan_call(me, moved, rate, amp, own_skip, ends, got)
    shifted = [gated] + [
        lax.ppermute(gated, "zh", [((n + d) % 4, n) for n in range(4)]) for d in (1, 2, 3)
    ]
    both = [lax.all_gather(g, "core", axis=0, tiled=False) for g in shifted]
    parts = project(jnp.stack([zh, zl]), weight, *both)
    return finish(lax.all_to_all(parts, "x", 0, 0, tiled=True))


def solution(mesh):
    fine = Mesh(mesh.devices.reshape(2, 8, 4, 4, 2), ("zl", "y", "x", "zh", "core"))
    seq, tensor = ("zl", "y", "x"), ("zh", "core")
    placed = (P(tensor, seq),) * 4 + (P(tensor, None), P(tensor, None), P(tensor))
    return jax.shard_map(
        per_device, mesh=fine, in_specs=placed, out_specs=P(tensor, seq), check_vma=False
    )
```

```python
import jax
import jax.numpy as jnp
from jax import lax
from jax.experimental import pallas as pl
from jax.experimental.pallas import tpu as pltpu
from jax.sharding import Mesh, PartitionSpec as P

MODES = 16
TOTAL = 16384
SPAN = 1024
CHUNKS = 8
STEP = SPAN // CHUNKS
WIDE = 128
BLOCK = 256
VMEM = pltpu.CompilerParams(vmem_limit_bytes=40 * 1024 * 1024)
F32 = jnp.float32
BF16 = jnp.bfloat16


def pack_kernel(q_hbm, k_hbm, v_hbm, out_hbm, q_ref, k_ref, v_ref, moved_ref, sems, out_sems):
    pairs = ((k_hbm, k_ref), (v_hbm, v_ref), (q_hbm, q_ref))
    copies = [pltpu.make_async_copy(*pair, sems.at[n]) for n, pair in enumerate(pairs)]
    for copy in copies:
        copy.start()
    copies[0].wait()
    copies[1].wait()
    leaving = []
    for n in range(8):
        j, begin = n % 4, BLOCK * (n // 4)
        if n == 4:
            copies[2].wait()
        rows, part = slice(WIDE * j, WIDE * (j + 1)), slice(begin, begin + BLOCK)
        moved_ref[j, part, :] = (k_ref[rows, :] * v_ref[rows, :] if n < 4 else q_ref[rows, :]).T
        leaving.append(pltpu.make_async_copy(moved_ref.at[j, part], out_hbm.at[j, part], out_sems.at[n]))
        leaving[-1].start()
    for copy in leaving:
        copy.wait()


def pack(q, k, v):
    return pl.pallas_call(
        pack_kernel,
        in_specs=[pl.BlockSpec(memory_space=pltpu.HBM)] * 3,
        out_specs=pl.BlockSpec(memory_space=pltpu.HBM),
        out_shape=jax.ShapeDtypeStruct((4, 2 * BLOCK, WIDE), BF16),
        scratch_shapes=[pltpu.VMEM((4 * WIDE, BLOCK), BF16)] * 3
        + [pltpu.VMEM((4, 2 * BLOCK, WIDE), BF16), pltpu.SemaphoreType.DMA((3,)), pltpu.SemaphoreType.DMA((8,))],
        compiler_params=pltpu.CompilerParams(vmem_limit_bytes=60 * 1024 * 1024),
        name="pack",
    )(q, k, v)


def load_product(moved_ref, p_ref):
    for j in range(4):
        p_ref[BLOCK * j : BLOCK * (j + 1), :] = moved_ref[j, 0:BLOCK, :].astype(F32)


def ends_kernel(moved_ref, rate_ref, ends_ref, total_ref, p_ref):
    load_product(moved_ref, p_ref)
    rate = rate_ref[...]
    ratio = jnp.exp(-rate)
    ratios = [jnp.broadcast_to(ratio[m : m + 1, :], (CHUNKS, WIDE)) for m in range(MODES)]

    def step(i, states):
        p = p_ref[pl.ds(i, CHUNKS, stride=STEP), :]
        return tuple(h * r + p for h, r in zip(states, ratios))

    zero = jnp.zeros((CHUNKS, WIDE), F32)
    states = lax.fori_loop(0, STEP, step, (zero,) * MODES, unroll=8)
    for m in range(MODES):
        ends_ref[pl.ds(m, CHUNKS, stride=MODES), :] = states[m]
    over_chunk = jnp.exp(-rate * STEP)
    total = ends_ref[0:MODES, :]
    for s in range(1, CHUNKS):
        total = total * over_chunk + ends_ref[MODES * s : MODES * (s + 1), :]
    total_ref[...] = total


def ends_call(moved, rate):
    return pl.pallas_call(
        ends_kernel,
        out_shape=[
            jax.ShapeDtypeStruct((CHUNKS * MODES, WIDE), F32),
            jax.ShapeDtypeStruct((MODES, WIDE), F32),
        ],
        scratch_shapes=[pltpu.VMEM((SPAN, WIDE), F32)],
        compiler_params=VMEM,
        name="ends",
    )(moved, rate)


def sent_kernel(total_ref, after_ref, out_ref):
    del after_ref
    for g in range(16):
        out_ref[g] = total_ref[...]


def sent_call(total, after):
    return pl.pallas_call(
        sent_kernel,
        in_specs=[pl.BlockSpec(memory_space=pltpu.VMEM), pl.BlockSpec(memory_space=pl.ANY)],
        out_shape=jax.ShapeDtypeStruct((16, MODES, WIDE), F32),
        compiler_params=VMEM,
        name="sent",
    )(total, after)


def scan_kernel(me_ref, moved_ref, rate_ref, amp_ref, skip_ref, ends_ref, got_ref, out_ref, p_ref, y_ref, first_ref):
    load_product(moved_ref, p_ref)
    rate = rate_ref[...]
    me = me_ref[0]
    over_span = jnp.exp(-rate * SPAN)
    over_chunk = jnp.exp(-rate * STEP)
    state = jnp.zeros((MODES, WIDE), F32)
    for g in range(16):
        state = jnp.where(g < me, state * over_span + got_ref[g], state)
    for s in range(CHUNKS):
        first_ref[MODES * s : MODES * (s + 1), :] = state
        state = state * over_chunk + ends_ref[MODES * s : MODES * (s + 1), :]
    ratio = jnp.exp(-rate)
    amp = amp_ref[...]
    spread = lambda x, m: jnp.broadcast_to(x[m : m + 1, :], (CHUNKS, WIDE))
    ratios = [spread(ratio, m) for m in range(MODES)]
    amps = [spread(amp, m) for m in range(MODES)]
    firsts = tuple(first_ref[pl.ds(m, CHUNKS, stride=MODES), :] for m in range(MODES))

    def step(i, states):
        p = p_ref[pl.ds(i, CHUNKS, stride=STEP), :]
        states = tuple(h * r + p for h, r in zip(states, ratios))
        terms = [h * a for h, a in zip(states, amps)]
        while len(terms) > 1:
            terms = [terms[n] + terms[n + 1] for n in range(0, len(terms), 2)]
        y_ref[pl.ds(i, CHUNKS, stride=STEP), :] = terms[0]
        return states

    lax.fori_loop(0, STEP, step, firsts, unroll=8)
    skip = skip_ref[...]
    for j in range(4):
        rows = slice(BLOCK * j, BLOCK * (j + 1))
        filtered = (y_ref[rows, :] + skip * p_ref[rows, :]).astype(BF16)
        gate = moved_ref[j, BLOCK : 2 * BLOCK, :].astype(F32)
        gated = (gate * filtered.astype(F32)).astype(BF16)
        out_ref[rows, :] = gated


def scan_call(me, moved, rate, amp, skip, ends, got):
    vmem = pl.BlockSpec(memory_space=pltpu.VMEM)
    return pl.pallas_call(
        scan_kernel,
        in_specs=[pl.BlockSpec(memory_space=pltpu.SMEM)] + [vmem] * 6,
        out_shape=jax.ShapeDtypeStruct((SPAN, WIDE), BF16),
        scratch_shapes=[
            pltpu.VMEM((SPAN, WIDE), F32),
            pltpu.VMEM((SPAN, WIDE), F32),
            pltpu.VMEM((CHUNKS * MODES, WIDE), F32),
        ],
        compiler_params=VMEM,
        name="scan",
    )(me, moved, rate, amp, skip, ends, got)


def copies_kernel(own_ref, far_ref, out_ref):
    for side, ref in enumerate((own_ref, far_ref)):
        for j in range(4):
            piece = ref[:, WIDE * j : WIDE * (j + 1)]
            for y in range(8):
                out_ref[4 * y + j, side] = piece


def copies_of(own, far):
    return pl.pallas_call(
        copies_kernel,
        out_shape=jax.ShapeDtypeStruct((32, 2, 64, WIDE), BF16),
        compiler_params=VMEM,
        name="copies",
    )(own, far)


def project_kernel(place_ref, w_ref, g0_ref, g1_ref, g2_ref, g3_ref, out_ref):
    zh, zl = place_ref[0], place_ref[1]
    half = SPAN // 2
    for h in range(2):
        for part in range(2):
            tokens = slice(half * part, half * (part + 1))
            total = jnp.zeros((256, half), F32)
            for d, g_ref in enumerate((g0_ref, g1_ref, g2_ref, g3_ref)):
                owner = lax.rem(zh + d, 4)
                weights, values = [], []
                for core in range(2):
                    t = 2 * owner + core
                    place, side = 2 * lax.rem(t, 4) + h, lax.rem(t // 4 + zl, 2)
                    weights.append(jnp.concatenate([w_ref[4 * place + n, side] for n in range(4)], axis=0))
                    values.append(g_ref[core, tokens, :])
                total += lax.dot_general(
                    jnp.concatenate(weights, axis=1),
                    jnp.concatenate(values, axis=1),
                    (((1,), (1,)), ((), ())),
                    preferred_element_type=F32,
                )
            for j in range(2):
                out_ref[2 * part + j, 256 * h : 256 * (h + 1), :] = total[:, BLOCK * j : BLOCK * (j + 1)].astype(BF16)


def project(place, w, *gated):
    vmem = pl.BlockSpec(memory_space=pltpu.VMEM)
    return pl.pallas_call(
        project_kernel,
        in_specs=[pl.BlockSpec(memory_space=pltpu.SMEM)] + [vmem] * 5,
        out_shape=jax.ShapeDtypeStruct((4, 512, BLOCK), BF16),
        compiler_params=VMEM,
        name="project",
    )(place, w, *gated)


def finish_kernel(parts_ref, out_ref):
    total = parts_ref[0].astype(F32)
    for n in range(1, 4):
        total += parts_ref[n].astype(F32)
    out_ref[...] = total.astype(BF16)


def finish(parts):
    return pl.pallas_call(
        finish_kernel,
        out_shape=jax.ShapeDtypeStruct((512, BLOCK), BF16),
        compiler_params=VMEM,
        name="finish",
    )(parts)


def place_weight(block):
    perm = []
    for zl in range(2):
        for y in range(8):
            for t in range(8):
                perm.append(((zl * 8 + y) * 8 + t, (2 * t + y % 2) * 8 + zl * 4 + y // 2))
    return lax.ppermute(block, ("zl", "y", "zh", "core"), perm)


def per_device(q, k, v, w, decay, residue, skip):
    x = lax.axis_index("x")
    zh, zl = lax.axis_index("zh"), lax.axis_index("zl")
    me = (zl * 8 + lax.axis_index("y")).reshape(1)
    own = place_weight(w.T)
    moved = lax.all_to_all(pack(q, k, v), "x", 0, 0, tiled=True)
    rate = lax.dynamic_slice_in_dim(decay, x * WIDE, WIDE, 0).T / TOTAL
    amp = lax.dynamic_slice_in_dim(residue, x * WIDE, WIDE, 0).T * jnp.sqrt(2.0 * rate)
    own_skip = lax.dynamic_slice_in_dim(skip, x * WIDE, WIDE, 0)[None]
    ends, total = ends_call(moved, rate)
    got = lax.all_to_all(sent_call(total, own), ("zl", "y"), 0, 0, tiled=True)
    far = lax.ppermute(own, "zl", [(0, 1), (1, 0)])
    weight = lax.all_to_all(copies_of(own, far), ("y", "x"), 0, 0, tiled=True)
    gated = scan_call(me, moved, rate, amp, own_skip, ends, got)
    shifted = [gated] + [
        lax.ppermute(gated, "zh", [((n + d) % 4, n) for n in range(4)]) for d in (1, 2, 3)
    ]
    both = [lax.all_gather(g, "core", axis=0, tiled=False) for g in shifted]
    parts = project(jnp.stack([zh, zl]), weight, *both)
    return finish(lax.all_to_all(parts, "x", 0, 0, tiled=True))


def solution(mesh):
    fine = Mesh(mesh.devices.reshape(2, 8, 4, 4, 2), ("zl", "y", "x", "zh", "core"))
    seq, tensor = ("zl", "y", "x"), ("zh", "core")
    placed = (P(tensor, seq),) * 4 + (P(tensor, None), P(tensor, None), P(tensor))
    return jax.shard_map(
        per_device, mesh=fine, in_specs=placed, out_specs=P(tensor, seq), check_vma=False
    )
```

```python
import jax
import jax.numpy as jnp
from jax import lax
from jax.experimental import pallas as pl
from jax.experimental.pallas import tpu as pltpu
from jax.sharding import Mesh, PartitionSpec as P

MODES = 16
TOTAL = 16384
SPAN = 1024
CHUNKS = 8
STEP = SPAN // CHUNKS
WIDE = 128
BLOCK = 256
VMEM = pltpu.CompilerParams(vmem_limit_bytes=40 * 1024 * 1024)
DISTANCES = (0, 2, 3, 1)
F32 = jnp.float32
BF16 = jnp.bfloat16


def pack_kernel(q_hbm, k_hbm, v_hbm, out_hbm, q_ref, k_ref, v_ref, moved_ref, sems, out_sems):
    pairs = ((k_hbm, k_ref), (v_hbm, v_ref), (q_hbm, q_ref))
    copies = [pltpu.make_async_copy(*pair, sems.at[n]) for n, pair in enumerate(pairs)]
    for copy in copies:
        copy.start()
    copies[0].wait()
    copies[1].wait()
    leaving = []
    for n in range(8):
        j, begin = n % 4, BLOCK * (n // 4)
        if n == 4:
            copies[2].wait()
        rows, part = slice(WIDE * j, WIDE * (j + 1)), slice(begin, begin + BLOCK)
        moved_ref[j, part, :] = (k_ref[rows, :] * v_ref[rows, :] if n < 4 else q_ref[rows, :]).T
        leaving.append(pltpu.make_async_copy(moved_ref.at[j, part], out_hbm.at[j, part], out_sems.at[n]))
        leaving[-1].start()
    for copy in leaving:
        copy.wait()


def pack(q, k, v):
    return pl.pallas_call(
        pack_kernel,
        in_specs=[pl.BlockSpec(memory_space=pltpu.HBM)] * 3,
        out_specs=pl.BlockSpec(memory_space=pltpu.HBM),
        out_shape=jax.ShapeDtypeStruct((4, 2 * BLOCK, WIDE), BF16),
        scratch_shapes=[pltpu.VMEM((4 * WIDE, BLOCK), BF16)] * 3
        + [pltpu.VMEM((4, 2 * BLOCK, WIDE), BF16), pltpu.SemaphoreType.DMA((3,)), pltpu.SemaphoreType.DMA((8,))],
        compiler_params=pltpu.CompilerParams(vmem_limit_bytes=60 * 1024 * 1024),
        name="pack",
    )(q, k, v)


def load_product(moved_ref, p_ref):
    for j in range(4):
        p_ref[BLOCK * j : BLOCK * (j + 1), :] = moved_ref[j, 0:BLOCK, :].astype(F32)


def ends_kernel(moved_ref, rate_ref, ends_ref, total_ref, p_ref):
    load_product(moved_ref, p_ref)
    rate = rate_ref[...]
    ratio = jnp.exp(-rate)
    ratios = [jnp.broadcast_to(ratio[m : m + 1, :], (CHUNKS, WIDE)) for m in range(MODES)]

    def step(i, states):
        p = p_ref[pl.ds(i, CHUNKS, stride=STEP), :]
        return tuple(h * r + p for h, r in zip(states, ratios))

    zero = jnp.zeros((CHUNKS, WIDE), F32)
    states = lax.fori_loop(0, STEP, step, (zero,) * MODES, unroll=8)
    for m in range(MODES):
        ends_ref[pl.ds(m, CHUNKS, stride=MODES), :] = states[m]
    over_chunk = jnp.exp(-rate * STEP)
    total = ends_ref[0:MODES, :]
    for s in range(1, CHUNKS):
        total = total * over_chunk + ends_ref[MODES * s : MODES * (s + 1), :]
    total_ref[...] = total


def ends_call(moved, rate):
    return pl.pallas_call(
        ends_kernel,
        out_shape=[
            jax.ShapeDtypeStruct((CHUNKS * MODES, WIDE), F32),
            jax.ShapeDtypeStruct((MODES, WIDE), F32),
        ],
        scratch_shapes=[pltpu.VMEM((SPAN, WIDE), F32)],
        compiler_params=VMEM,
        name="ends",
    )(moved, rate)


def sent_kernel(total_ref, after_ref, out_ref):
    del after_ref
    for g in range(16):
        out_ref[g] = total_ref[...]


def sent_call(total, after):
    return pl.pallas_call(
        sent_kernel,
        in_specs=[pl.BlockSpec(memory_space=pltpu.VMEM), pl.BlockSpec(memory_space=pl.ANY)],
        out_shape=jax.ShapeDtypeStruct((16, MODES, WIDE), F32),
        compiler_params=VMEM,
        name="sent",
    )(total, after)


def scan_kernel(me_ref, moved_ref, rate_ref, amp_ref, skip_ref, ends_ref, got_ref, out_ref, p_ref, y_ref, first_ref):
    load_product(moved_ref, p_ref)
    rate = rate_ref[...]
    me = me_ref[0]
    over_span = jnp.exp(-rate * SPAN)
    over_chunk = jnp.exp(-rate * STEP)
    state = jnp.zeros((MODES, WIDE), F32)
    for g in range(16):
        state = jnp.where(g < me, state * over_span + got_ref[g], state)
    for s in range(CHUNKS):
        first_ref[MODES * s : MODES * (s + 1), :] = state
        state = state * over_chunk + ends_ref[MODES * s : MODES * (s + 1), :]
    ratio = jnp.exp(-rate)
    amp = amp_ref[...]
    spread = lambda x, m: jnp.broadcast_to(x[m : m + 1, :], (CHUNKS, WIDE))
    ratios = [spread(ratio, m) for m in range(MODES)]
    amps = [spread(amp, m) for m in range(MODES)]
    firsts = tuple(first_ref[pl.ds(m, CHUNKS, stride=MODES), :] for m in range(MODES))

    def step(i, states):
        p = p_ref[pl.ds(i, CHUNKS, stride=STEP), :]
        states = tuple(h * r + p for h, r in zip(states, ratios))
        terms = [h * a for h, a in zip(states, amps)]
        while len(terms) > 1:
            terms = [terms[n] + terms[n + 1] for n in range(0, len(terms), 2)]
        y_ref[pl.ds(i, CHUNKS, stride=STEP), :] = terms[0]
        return states

    lax.fori_loop(0, STEP, step, firsts, unroll=8)
    skip = skip_ref[...]
    for j in range(4):
        rows = slice(BLOCK * j, BLOCK * (j + 1))
        filtered = (y_ref[rows, :] + skip * p_ref[rows, :]).astype(BF16)
        gate = moved_ref[j, BLOCK : 2 * BLOCK, :].astype(F32)
        gated = (gate * filtered.astype(F32)).astype(BF16)
        out_ref[rows, :] = gated


def scan_call(me, moved, rate, amp, skip, ends, got):
    vmem = pl.BlockSpec(memory_space=pltpu.VMEM)
    return pl.pallas_call(
        scan_kernel,
        in_specs=[pl.BlockSpec(memory_space=pltpu.SMEM)] + [vmem] * 6,
        out_shape=jax.ShapeDtypeStruct((SPAN, WIDE), BF16),
        scratch_shapes=[
            pltpu.VMEM((SPAN, WIDE), F32),
            pltpu.VMEM((SPAN, WIDE), F32),
            pltpu.VMEM((CHUNKS * MODES, WIDE), F32),
        ],
        compiler_params=VMEM,
        name="scan",
    )(me, moved, rate, amp, skip, ends, got)


def copies_kernel(own_ref, far_ref, out_ref):
    for side, ref in enumerate((own_ref, far_ref)):
        for j in range(4):
            piece = ref[:, WIDE * j : WIDE * (j + 1)]
            for y in range(8):
                out_ref[4 * y + j, side] = piece


def copies_of(own, far):
    return pl.pallas_call(
        copies_kernel,
        out_shape=jax.ShapeDtypeStruct((32, 2, 64, WIDE), BF16),
        compiler_params=VMEM,
        name="copies",
    )(own, far)


def project_kernel(place_ref, w_ref, g0_ref, g1_ref, g2_ref, g3_ref, out_ref):
    zh, zl = place_ref[0], place_ref[1]
    half = SPAN // 2
    for h in range(2):
        for part in range(2):
            tokens = slice(half * part, half * (part + 1))
            total = jnp.zeros((256, half), F32)
            for d, g_ref in zip(DISTANCES, (g0_ref, g1_ref, g2_ref, g3_ref)):
                owner = lax.rem(zh + d, 4)
                weights, values = [], []
                for core in range(2):
                    t = 2 * owner + core
                    place, side = 2 * lax.rem(t, 4) + h, lax.rem(t // 4 + zl, 2)
                    weights.append(jnp.concatenate([w_ref[4 * place + n, side] for n in range(4)], axis=0))
                    values.append(g_ref[core, tokens, :])
                total += lax.dot_general(
                    jnp.concatenate(weights, axis=1),
                    jnp.concatenate(values, axis=1),
                    (((1,), (1,)), ((), ())),
                    preferred_element_type=F32,
                )
            for j in range(2):
                out_ref[2 * part + j, 256 * h : 256 * (h + 1), :] = total[:, BLOCK * j : BLOCK * (j + 1)].astype(BF16)


def project(place, w, *gated):
    vmem = pl.BlockSpec(memory_space=pltpu.VMEM)
    return pl.pallas_call(
        project_kernel,
        in_specs=[pl.BlockSpec(memory_space=pltpu.SMEM)] + [vmem] * 5,
        out_shape=jax.ShapeDtypeStruct((4, 512, BLOCK), BF16),
        compiler_params=VMEM,
        name="project",
    )(place, w, *gated)


def finish_kernel(parts_ref, out_ref):
    total = parts_ref[0].astype(F32)
    for n in range(1, 4):
        total += parts_ref[n].astype(F32)
    out_ref[...] = total.astype(BF16)


def finish(parts):
    return pl.pallas_call(
        finish_kernel,
        out_shape=jax.ShapeDtypeStruct((512, BLOCK), BF16),
        compiler_params=VMEM,
        name="finish",
    )(parts)


def place_weight(block):
    perm = []
    for zl in range(2):
        for y in range(8):
            for t in range(8):
                perm.append(((zl * 8 + y) * 8 + t, (2 * t + y % 2) * 8 + zl * 4 + y // 2))
    return lax.ppermute(block, ("zl", "y", "zh", "core"), perm)


def per_device(q, k, v, w, decay, residue, skip):
    x = lax.axis_index("x")
    zh, zl = lax.axis_index("zh"), lax.axis_index("zl")
    me = (zl * 8 + lax.axis_index("y")).reshape(1)
    own = place_weight(w.T)
    moved = lax.all_to_all(pack(q, k, v), "x", 0, 0, tiled=True)
    rate = lax.dynamic_slice_in_dim(decay, x * WIDE, WIDE, 0).T / TOTAL
    amp = lax.dynamic_slice_in_dim(residue, x * WIDE, WIDE, 0).T * jnp.sqrt(2.0 * rate)
    own_skip = lax.dynamic_slice_in_dim(skip, x * WIDE, WIDE, 0)[None]
    ends, total = ends_call(moved, rate)
    got = lax.all_to_all(sent_call(total, own), ("zl", "y"), 0, 0, tiled=True)
    far = lax.ppermute(own, "zl", [(0, 1), (1, 0)])
    weight = lax.all_to_all(copies_of(own, far), ("y", "x"), 0, 0, tiled=True)
    gated = scan_call(me, moved, rate, amp, own_skip, ends, got)
    shifted = [gated] + [
        lax.ppermute(gated, "zh", [((n + d) % 4, n) for n in range(4)]) for d in DISTANCES[1:]
    ]
    both = [lax.all_gather(g, "core", axis=0, tiled=False) for g in shifted]
    parts = project(jnp.stack([zh, zl]), weight, *both)
    return finish(lax.all_to_all(parts, "x", 0, 0, tiled=True))


def solution(mesh):
    fine = Mesh(mesh.devices.reshape(2, 8, 4, 4, 2), ("zl", "y", "x", "zh", "core"))
    seq, tensor = ("zl", "y", "x"), ("zh", "core")
    placed = (P(tensor, seq),) * 4 + (P(tensor, None), P(tensor, None), P(tensor))
    return jax.shard_map(
        per_device, mesh=fine, in_specs=placed, out_specs=P(tensor, seq), check_vma=False
    )
```

```python
import jax
import jax.numpy as jnp
from jax import lax
from jax.experimental import pallas as pl
from jax.experimental.pallas import tpu as pltpu
from jax.sharding import Mesh, PartitionSpec as P

MODES = 16
TOTAL = 16384
SPAN = 1024
CHUNKS = 8
STEP = SPAN // CHUNKS
WIDE = 128
BLOCK = 256
VMEM = pltpu.CompilerParams(vmem_limit_bytes=40 * 1024 * 1024)
DISTANCES = (0, 2, 3, 1)
F32 = jnp.float32
BF16 = jnp.bfloat16


def pack_kernel(q_hbm, k_hbm, v_hbm, out_hbm, q_ref, k_ref, v_ref, moved_ref, sems, out_sems):
    pairs = ((k_hbm, k_ref), (v_hbm, v_ref), (q_hbm, q_ref))
    copies = [pltpu.make_async_copy(*pair, sems.at[n]) for n, pair in enumerate(pairs)]
    for copy in copies:
        copy.start()
    copies[0].wait()
    copies[1].wait()
    leaving = []
    for n in range(8):
        j, begin = n % 4, BLOCK * (n // 4)
        if n == 4:
            copies[2].wait()
        rows, part = slice(WIDE * j, WIDE * (j + 1)), slice(begin, begin + BLOCK)
        moved_ref[j, part, :] = (k_ref[rows, :] * v_ref[rows, :] if n < 4 else q_ref[rows, :]).T
        leaving.append(pltpu.make_async_copy(moved_ref.at[j, part], out_hbm.at[j, part], out_sems.at[n]))
        leaving[-1].start()
    for copy in leaving:
        copy.wait()


def pack(q, k, v):
    return pl.pallas_call(
        pack_kernel,
        in_specs=[pl.BlockSpec(memory_space=pltpu.HBM)] * 3,
        out_specs=pl.BlockSpec(memory_space=pltpu.HBM),
        out_shape=jax.ShapeDtypeStruct((4, 2 * BLOCK, WIDE), BF16),
        scratch_shapes=[pltpu.VMEM((4 * WIDE, BLOCK), BF16)] * 3
        + [pltpu.VMEM((4, 2 * BLOCK, WIDE), BF16), pltpu.SemaphoreType.DMA((3,)), pltpu.SemaphoreType.DMA((8,))],
        compiler_params=pltpu.CompilerParams(vmem_limit_bytes=60 * 1024 * 1024),
        name="pack",
    )(q, k, v)


def load_product(moved_ref, p_ref):
    for j in range(4):
        p_ref[BLOCK * j : BLOCK * (j + 1), :] = moved_ref[j, 0:BLOCK, :].astype(F32)


def ends_kernel(moved_ref, rate_ref, ends_ref, total_ref, p_ref):
    load_product(moved_ref, p_ref)
    rate = rate_ref[...]
    ratio = jnp.exp(-rate)
    ratios = [jnp.broadcast_to(ratio[m : m + 1, :], (CHUNKS, WIDE)) for m in range(MODES)]

    def step(i, states):
        p = p_ref[pl.ds(i, CHUNKS, stride=STEP), :]
        return tuple(h * r + p for h, r in zip(states, ratios))

    zero = jnp.zeros((CHUNKS, WIDE), F32)
    states = lax.fori_loop(0, STEP, step, (zero,) * MODES, unroll=8)
    for m in range(MODES):
        ends_ref[pl.ds(m, CHUNKS, stride=MODES), :] = states[m]
    over_chunk = jnp.exp(-rate * STEP)
    total = ends_ref[0:MODES, :]
    for s in range(1, CHUNKS):
        total = total * over_chunk + ends_ref[MODES * s : MODES * (s + 1), :]
    total_ref[...] = total


def ends_call(moved, rate):
    return pl.pallas_call(
        ends_kernel,
        out_shape=[
            jax.ShapeDtypeStruct((CHUNKS * MODES, WIDE), F32),
            jax.ShapeDtypeStruct((MODES, WIDE), F32),
        ],
        scratch_shapes=[pltpu.VMEM((SPAN, WIDE), F32)],
        compiler_params=VMEM,
        name="ends",
    )(moved, rate)


def sent_kernel(total_ref, after_ref, out_ref):
    del after_ref
    for g in range(16):
        out_ref[g] = total_ref[...]


def sent_call(total, after):
    return pl.pallas_call(
        sent_kernel,
        in_specs=[pl.BlockSpec(memory_space=pltpu.VMEM), pl.BlockSpec(memory_space=pl.ANY)],
        out_shape=jax.ShapeDtypeStruct((16, MODES, WIDE), F32),
        compiler_params=VMEM,
        name="sent",
    )(total, after)


def scan_kernel(me_ref, moved_ref, rate_ref, amp_ref, skip_ref, ends_ref, got_ref, out_ref, p_ref, y_ref, first_ref):
    load_product(moved_ref, p_ref)
    rate = rate_ref[...]
    me = me_ref[0]
    over_span = jnp.exp(-rate * SPAN)
    over_chunk = jnp.exp(-rate * STEP)
    state = jnp.zeros((MODES, WIDE), F32)
    for g in range(16):
        state = jnp.where(g < me, state * over_span + got_ref[g], state)
    for s in range(CHUNKS):
        first_ref[MODES * s : MODES * (s + 1), :] = state
        state = state * over_chunk + ends_ref[MODES * s : MODES * (s + 1), :]
    ratio = jnp.exp(-rate)
    amp = amp_ref[...]
    spread = lambda x, m: jnp.broadcast_to(x[m : m + 1, :], (CHUNKS, WIDE))
    ratios = [spread(ratio, m) for m in range(MODES)]
    amps = [spread(amp, m) for m in range(MODES)]
    firsts = tuple(first_ref[pl.ds(m, CHUNKS, stride=MODES), :] for m in range(MODES))

    def step(i, states):
        p = p_ref[pl.ds(i, CHUNKS, stride=STEP), :]
        states = tuple(h * r + p for h, r in zip(states, ratios))
        terms = [h * a for h, a in zip(states, amps)]
        while len(terms) > 1:
            terms = [terms[n] + terms[n + 1] for n in range(0, len(terms), 2)]
        y_ref[pl.ds(i, CHUNKS, stride=STEP), :] = terms[0]
        return states

    lax.fori_loop(0, STEP, step, firsts, unroll=8)
    skip = skip_ref[...]
    for j in range(4):
        rows = slice(BLOCK * j, BLOCK * (j + 1))
        filtered = (y_ref[rows, :] + skip * p_ref[rows, :]).astype(BF16)
        gate = moved_ref[j, BLOCK : 2 * BLOCK, :].astype(F32)
        gated = (gate * filtered.astype(F32)).astype(BF16)
        out_ref[rows, :] = gated


def scan_call(me, moved, rate, amp, skip, ends, got):
    vmem = pl.BlockSpec(memory_space=pltpu.VMEM)
    return pl.pallas_call(
        scan_kernel,
        in_specs=[pl.BlockSpec(memory_space=pltpu.SMEM)] + [vmem] * 6,
        out_shape=jax.ShapeDtypeStruct((SPAN, WIDE), BF16),
        scratch_shapes=[
            pltpu.VMEM((SPAN, WIDE), F32),
            pltpu.VMEM((SPAN, WIDE), F32),
            pltpu.VMEM((CHUNKS * MODES, WIDE), F32),
        ],
        compiler_params=VMEM,
        name="scan",
    )(me, moved, rate, amp, skip, ends, got)


def copies_kernel(own_ref, far_ref, out_ref):
    for side, ref in enumerate((own_ref, far_ref)):
        for j in range(4):
            piece = ref[:, WIDE * j : WIDE * (j + 1)]
            for y in range(8):
                out_ref[8 * j + y, side] = piece


def copies_of(own, far):
    return pl.pallas_call(
        copies_kernel,
        out_shape=jax.ShapeDtypeStruct((32, 2, 64, WIDE), BF16),
        compiler_params=VMEM,
        name="copies",
    )(own, far)


def project_kernel(place_ref, w_ref, g0_ref, g1_ref, g2_ref, g3_ref, out_ref):
    zh, zl = place_ref[0], place_ref[1]
    half = SPAN // 2
    for h in range(2):
        for part in range(2):
            tokens = slice(half * part, half * (part + 1))
            total = jnp.zeros((256, half), F32)
            for d, g_ref in zip(DISTANCES, (g0_ref, g1_ref, g2_ref, g3_ref)):
                owner = lax.rem(zh + d, 4)
                weights, values = [], []
                for core in range(2):
                    t = 2 * owner + core
                    place, side = 2 * lax.rem(t, 4) + h, lax.rem(t // 4 + zl, 2)
                    weights.append(jnp.concatenate([w_ref[8 * n + place, side] for n in range(4)], axis=0))
                    values.append(g_ref[core, tokens, :])
                total += lax.dot_general(
                    jnp.concatenate(weights, axis=1),
                    jnp.concatenate(values, axis=1),
                    (((1,), (1,)), ((), ())),
                    preferred_element_type=F32,
                )
            for j in range(2):
                out_ref[2 * part + j, 256 * h : 256 * (h + 1), :] = total[:, BLOCK * j : BLOCK * (j + 1)].astype(BF16)


def project(place, w, *gated):
    vmem = pl.BlockSpec(memory_space=pltpu.VMEM)
    return pl.pallas_call(
        project_kernel,
        in_specs=[pl.BlockSpec(memory_space=pltpu.SMEM)] + [vmem] * 5,
        out_shape=jax.ShapeDtypeStruct((4, 512, BLOCK), BF16),
        compiler_params=VMEM,
        name="project",
    )(place, w, *gated)


def finish_kernel(parts_ref, out_ref):
    total = parts_ref[0].astype(F32)
    for n in range(1, 4):
        total += parts_ref[n].astype(F32)
    out_ref[...] = total.astype(BF16)


def finish(parts):
    return pl.pallas_call(
        finish_kernel,
        out_shape=jax.ShapeDtypeStruct((512, BLOCK), BF16),
        compiler_params=VMEM,
        name="finish",
    )(parts)


def place_weight(block):
    perm = []
    for zl in range(2):
        for y in range(8):
            for t in range(8):
                perm.append(((zl * 8 + y) * 8 + t, (2 * t + y % 2) * 8 + zl * 4 + y // 2))
    return lax.ppermute(block, ("zl", "y", "zh", "core"), perm)


def per_device(q, k, v, w, decay, residue, skip):
    x = lax.axis_index("x")
    zh, zl = lax.axis_index("zh"), lax.axis_index("zl")
    me = (zl * 8 + lax.axis_index("y")).reshape(1)
    own = place_weight(w.T)
    moved = lax.all_to_all(pack(q, k, v), "x", 0, 0, tiled=True)
    rate = lax.dynamic_slice_in_dim(decay, x * WIDE, WIDE, 0).T / TOTAL
    amp = lax.dynamic_slice_in_dim(residue, x * WIDE, WIDE, 0).T * jnp.sqrt(2.0 * rate)
    own_skip = lax.dynamic_slice_in_dim(skip, x * WIDE, WIDE, 0)[None]
    ends, total = ends_call(moved, rate)
    got = lax.all_to_all(sent_call(total, own), ("zl", "y"), 0, 0, tiled=True)
    far = lax.ppermute(own, "zl", [(0, 1), (1, 0)])
    weight = lax.all_to_all(copies_of(own, far), ("x", "y"), 0, 0, tiled=True)
    gated = scan_call(me, moved, rate, amp, own_skip, ends, got)
    shifted = [gated] + [
        lax.ppermute(gated, "zh", [((n + d) % 4, n) for n in range(4)]) for d in DISTANCES[1:]
    ]
    both = [lax.all_gather(g, "core", axis=0, tiled=False) for g in shifted]
    parts = project(jnp.stack([zh, zl]), weight, *both)
    return finish(lax.all_to_all(parts, "x", 0, 0, tiled=True))


def solution(mesh):
    fine = Mesh(mesh.devices.reshape(2, 8, 4, 4, 2), ("zl", "y", "x", "zh", "core"))
    seq, tensor = ("zl", "y", "x"), ("zh", "core")
    placed = (P(tensor, seq),) * 4 + (P(tensor, None), P(tensor, None), P(tensor))
    return jax.shard_map(
        per_device, mesh=fine, in_specs=placed, out_specs=P(tensor, seq), check_vma=False
    )
```
